512 devices in a mesh: layer: 2 (over x_lo), row: 16 (over y, x_hi, core), col: 16 (over z).
Axes of the slice: x: 4 (x_hi: 2, x_lo: 2; x = x_hi * 2 + x_lo), y: 4, z: 16, core: 2. Of those that a mesh axis runs over, the one named last changes fastest.
Arguments:
- x_blocks: bfloat16 [16, 16, 32, 128, 128], P('col', 'row'), may hold values from -1.5 to 1.5
- x_coords: int32 [16, 16, 2, 32], P('col', 'row'), may hold values from -1 to 127, as said below
Outputs:
- c_blocks: float32 [16, 16, 32, 128, 128], P('col', 'row', 'layer')
The draws below stay inside these ranges and needn't reach their ends.
Inputs may be any that keep to these rules, and one draw needn't show every extreme that they name: `x_coords`: each band b has one set of 8 block rows used in it: every non-empty slot of a tile (I, J) has its block row in the set of band I and its block column in the set of band J, and every tile uses all 8 rows of its set and all 8 columns of its set. No block appears twice in a tile. Non-empty slots come first; each tile has 8 to 32 of them, and some tile has 32.
All inputs are finite; a program needn't handle non-finite values.
Results may differ from the reference program's by a relative error of at most 0.0003.
Values may be sent and summed in bfloat16 or wider, within the bound.
No kernel may reach another device: no remote copies, remote signals or barrier semaphores. Data moves between devices by JAX's collectives and lax.ppermute only.
A program may use at most 64 MiB of HBM per device.

```python
import jax
import jax.numpy as jnp
from jax import lax

BLK = 128
BT = 128
H = 8
P_SIZE = 32
BANDS = 16
TERMS = 4


def draw_x_coords(key, part):
    key = jax.random.fold_in(key, 11)
    band_keys = jax.random.split(jax.random.fold_in(key, 1), BANDS)

    def band_rows(band_key):
        return jax.random.permutation(band_key, BT)[:H].astype(jnp.int32)
    active = jax.vmap(band_rows)(band_keys)
    tile_total = BANDS * BANDS
    counts = jax.random.randint(jax.random.fold_in(key, 2), (tile_total,), H, P_SIZE + 1).astype(jnp.int32)
    full_tile = jax.random.randint(jax.random.fold_in(key, 3), (), 0, tile_total)
    counts = jnp.where(jnp.arange(tile_total) == full_tile, P_SIZE, counts).astype(jnp.int32)
    tile_keys = jax.random.split(jax.random.fold_in(key, 4), tile_total)

    def one_tile(tile_key, flat_at, count_at):
        band_i = flat_at // BANDS
        band_j = flat_at % BANDS
        paired = jax.random.permutation(jax.random.fold_in(tile_key, 1), H).astype(jnp.int32)
        scores = jax.random.permutation(jax.random.fold_in(tile_key, 2), H * H).astype(jnp.int32)
        slot_rows = jnp.arange(H * H, dtype=jnp.int32) // H
        slot_cols = jnp.arange(H * H, dtype=jnp.int32) % H
        on_pair = slot_cols == paired[slot_rows]
        scores = scores + H * H * on_pair.astype(jnp.int32)
        ranking = jnp.argsort(-scores, stable=True)[:P_SIZE]
        row_of = active[band_i][slot_rows[ranking]]
        col_of = active[band_j][slot_cols[ranking]]
        live = jnp.arange(P_SIZE) < count_at
        return jnp.stack([jnp.where(live, row_of, -1), jnp.where(live, col_of, -1)]).astype(jnp.int32)
    result = jax.vmap(one_tile)(tile_keys, jnp.arange(tile_total, dtype=jnp.int32), counts)
    return result.reshape(BANDS, BANDS, 2, P_SIZE)


def block_scale(rng, shape, pieces, least, top_value):
    factor_of, own = 1.0, jax.random.fold_in(rng, 6)
    for dim, shards_of in pieces:
        heights = jnp.exp(jax.random.uniform(jax.random.fold_in(own, dim), (shards_of,), jnp.float32, least / len(pieces), top_value / len(pieces)))
        factor_of = factor_of * jnp.repeat(heights, shape[dim] // shards_of).reshape([-1 if axis == dim else 1 for axis in range(len(shape))])
    return factor_of


def noise(key, dims, scale, reach, pieces=(), kind=jnp.bfloat16):
    values = scale * jax.random.normal(key, dims, jnp.float32)
    if pieces:
        values = values * block_scale(key, dims, pieces, -0.22, 0.18)
    return jnp.clip(values, -reach, reach).astype(kind)


def setup_inputs(seed: int = 0) -> dict:
    streams_of = jax.random.split(jax.random.key(seed), 3)
    return {
        "x_blocks": noise(streams_of[0], (BANDS, BANDS, P_SIZE, BLK, BLK), 0.25, 1.5, ((0, 16), (1, 16))),
        "x_coords": draw_x_coords(jax.random.fold_in(streams_of[2], 71), 0),
    }


def pair_list(a_coords, b_coords, o_coords):
    slot_count = a_coords.shape[1]
    matches = (a_coords[1][:, None] == b_coords[0][None, :]) & (a_coords[0][:, None] >= 0) & (b_coords[0][None, :] >= 0)
    ranking = jnp.argsort(1 - matches.astype(jnp.int32), axis=1, stable=True)[:, :H]
    partner = ranking.reshape(-1).astype(jnp.int32)
    usable = jnp.take_along_axis(matches, ranking, axis=1).reshape(-1)
    source = jnp.repeat(jnp.arange(slot_count, dtype=jnp.int32), H)
    row_need = a_coords[0][source]
    col_need = b_coords[1][partner]
    landing = (o_coords[0][None, :] == row_need[:, None]) & (o_coords[1][None, :] == col_need[:, None]) & (o_coords[0][None, :] >= 0)
    slot_at = jnp.sum(landing.astype(jnp.int32) * jnp.arange(slot_count, dtype=jnp.int32)[None, :], axis=1).astype(jnp.int32)
    located = jnp.any(landing, axis=1)
    target = jnp.where(usable & located, slot_at, slot_count).astype(jnp.int32)
    return source, partner, target


def tile_product(a_blocks, a_coords, b_blocks, b_coords, o_coords):
    slot_count = a_coords.shape[1]
    source, partner, target = pair_list(a_coords, b_coords, o_coords)
    pair_total = source.shape[0]
    group_rows = min(64, pair_total)
    summed = jnp.zeros((slot_count + 1, a_blocks.shape[1], a_blocks.shape[2]), jnp.float32)
    for group_at in range(pair_total // group_rows):
        lower = group_at * group_rows
        left_part = a_blocks[source[lower:lower + group_rows]].astype(jnp.float32)
        right_part = b_blocks[partner[lower:lower + group_rows]].astype(jnp.float32)
        product = jnp.einsum("mij,mjk->mik", left_part, right_part, precision=lax.Precision.HIGHEST)
        summed = summed + jax.ops.segment_sum(product, target[lower:lower + group_rows], num_segments=slot_count + 1)
    return summed[:slot_count]


def reference(x_blocks, x_coords):
    def one_tile(flat_at):
        band_i = flat_at // BANDS
        band_j = flat_at % BANDS

        def add_term(step_at, summed):
            band_k = (band_i + step_at) % BANDS
            return summed + tile_product(x_blocks[band_i, band_k], x_coords[band_i, band_k], x_blocks[band_k, band_j], x_coords[band_k, band_j], x_coords[band_i, band_j])

        return lax.fori_loop(0, TERMS, add_term, jnp.zeros((P_SIZE, BLK, BLK), jnp.float32))

    result = lax.map(one_tile, jnp.arange(BANDS * BANDS, dtype=jnp.int32))
    return result.reshape(BANDS, BANDS, P_SIZE, BLK, BLK)
```

```python
import functools

import jax
import jax.numpy as jnp
from jax import lax
from jax.experimental import pallas as pl
from jax.experimental.pallas import tpu as pltpu
from jax.sharding import PartitionSpec as P

H = 8
STEPS = 4
W = 128
GROUP = 8
ROWS = GROUP * W
PACK = ROWS + 16
DENSE = H * W
AXES = ("layer", "row", "col")


def pairs_of(mesh_shape, target):
    layers, rows, cols = mesh_shape
    flat = lambda at: (at[0] * rows + at[1]) * cols + at[2]
    found = []
    for l in range(layers):
        for r in range(rows):
            for c in range(cols):
                to = target(l, r, c)
                if to is not None:
                    found.append((flat((l, r, c)), flat(to)))
    return found


def cells_and_table(coords):
    slots = coords.shape[1]
    values = jnp.arange(W, dtype=jnp.int32)
    used = jnp.any(coords[:, :, None] == values[None, None, :], axis=1)
    below = used[:, None, :] & (values[None, None, :] < coords[:, :, None])
    rank = jnp.sum(below.astype(jnp.int32), axis=2)
    cells = jnp.where(coords[0] >= 0, rank[0] * H + rank[1], H * H)
    hits = cells[None, :] == values[:, None]
    order = jnp.arange(slots, dtype=jnp.int32) - slots
    table = slots + jnp.sum(jnp.where(hits, order[None, :], 0), axis=1)
    return cells, table


def kernel(own_table, own_cells, meta, own, *refs):
    n_left = 10
    left = refs[:n_left]
    right = refs[n_left:n_left + 12]
    out = refs[n_left + 12]
    (a_all, b_all, a_head, b_head, table_v, table_s, a_dense, b_dense, prod, sems) = refs[n_left + 13:]
    copies = []

    def start(src, dst):
        c = pltpu.make_async_copy(src, dst, sems.at[len(copies)])
        c.start()
        copies.append(c)

    at = 0
    for ref in left:
        for e in range(ref.shape[0]):
            place = meta[at]
            step, part = place // 4, place % 4
            start(ref.at[e, pl.ds(0, ROWS)], a_all.at[step, pl.ds(part * ROWS, ROWS)])
            start(ref.at[e, pl.ds(ROWS, 16)], a_head.at[place])
            at += 1
    start(own, b_all.at[0, pl.ds(0, 4 * ROWS)])
    for s in range(1, STEPS):
        for g in range(4):
            place = meta[16 + g]
            ref = right[(s - 1) * 4 + g]
            start(ref.at[pl.ds(0, ROWS)], b_all.at[s, pl.ds(place * ROWS, ROWS)])
            start(ref.at[pl.ds(ROWS, 16)], b_head.at[(s - 1) * 4 + place])
    zero = jnp.zeros((W, W), jnp.bfloat16)
    for s in range(STEPS):
        a_all[s, 4 * ROWS:, :] = zero
        b_all[s, 4 * ROWS:, :] = zero
    for c in copies:
        c.wait()
    for s in range(STEPS):
        table_v[s:s + 1, :] = a_head[4 * s, 0:1, :].astype(jnp.float32).astype(jnp.int32)
        if s:
            table_v[4 + s:5 + s, :] = b_head[4 * (s - 1), 0:1, :].astype(jnp.float32).astype(jnp.int32)
        else:
            table_v[4:5, :] = jnp.zeros((1, W), jnp.int32)
    last = pltpu.make_async_copy(table_v, table_s, sems.at[len(copies)])
    last.start()
    last.wait()

    @pl.loop(0, W)
    def _(i):
        table_s[4, i] = own_table[i]

    @pl.loop(0, STEPS)
    def _(s):
        for r in range(H):
            for k in range(H):
                slot = table_s[s, r * H + k]
                rows = pl.ds(pl.multiple_of(slot * W, W), W)
                a_dense[s, r * W:(r + 1) * W, k * W:(k + 1) * W] = a_all[s, rows, :]
                slot = table_s[4 + s, r * H + k]
                rows = pl.ds(pl.multiple_of(slot * W, W), W)
                b_dense[s, k // 2, r * W:(r + 1) * W, (k % 2) * W:(k % 2 + 1) * W] = b_all[s, rows, :]

    @pl.loop(0, 4)
    def _(n):
        total = jnp.dot(a_dense[0], b_dense[0, n], preferred_element_type=jnp.float32)
        for s in range(1, STEPS):
            total += jnp.dot(a_dense[s], b_dense[s, n], preferred_element_type=jnp.float32)
        prod[2 * n] = total[:, :W]
        prod[2 * n + 1] = total[:, W:]

    base = meta[20]

    @pl.loop(0, 16)
    def _(q):
        cell = own_cells[base + q]
        live = cell < H * H
        held = jnp.where(live, cell, 0)
        rows = pl.ds(pl.multiple_of((held // H) * W, W), W)
        block = prod[held % H, rows, :]
        out[q] = jnp.where(live, block, jnp.zeros_like(block))


def body(mesh_shape, x_blocks, x_coords):
    blocks = x_blocks[0, 0].reshape(4, ROWS, W)
    coords = x_coords[0, 0]
    _, rows, cols = mesh_shape
    layer, row, col = (lax.axis_index(a) for a in AXES)
    cells, table = cells_and_table(coords)
    head = jnp.broadcast_to(table.astype(jnp.bfloat16)[None, None, :], (4, 16, W))
    packed = jnp.concatenate([blocks, head], axis=1)

    def send(value, target):
        return lax.ppermute(value, AXES, pairs_of(mesh_shape, target))

    down = lambda l, r, c: (l, r, (c - 1) % cols)
    over = lambda l, r, c: (1 - l, r, c)
    mine = lax.dynamic_slice_in_dim(packed, 2 * layer, 2, 0)
    chunk = [mine[0], mine[1]]
    right = []
    for s in range(1, STEPS):
        chunk = [send(v, down) for v in chunk]
        right += chunk + [send(v, over) for v in chunk]

    place = (row - col) % rows
    part_at = place // 4
    piece = packed[0]
    for t in range(1, 4):
        got = send(packed[t], lambda l, r, c: (l, (r + 4 * t) % rows, c) if (r - c) % rows < 4 else None)
        piece = jnp.where(part_at == t, got, piece)
    cross = send(piece, lambda l, r, c: (1 - l, r ^ 2, c))
    here = jnp.stack([piece, cross])
    y_up = lambda l, r, c: (l, (r + 4) % rows, c)
    y_dn = lambda l, r, c: (l, (r - 4) % rows, c)
    from_dn = send(here, y_up)
    from_up = send(here, y_dn)
    far0 = send(from_up[0], y_dn)
    far1 = send(from_dn[1], y_up)
    left = [here, from_dn, from_up, far0[None], far1[None]]
    twin = lambda l, r, c: (l, r ^ 1, c)
    left += [send(v, twin) for v in left]
    places = []
    for me in (row, row ^ 1):
        for r, es in ((me, (0, 1)), ((me - 4) % rows, (0, 1)), ((me + 4) % rows, (0, 1)), ((me + 8) % rows, (0, 1))):
            for e in es:
                d = ((r ^ 2 if e else r) - col) % rows
                places.append((d % 4) * 4 + d // 4)
    own_half, other_half = 2 * layer, 2 * (1 - layer)
    meta = jnp.stack(places + [own_half, own_half + 1, other_half, other_half + 1, 16 * layer]).astype(jnp.int32)

    any_space = pl.BlockSpec(memory_space=pl.ANY)
    smem = pl.BlockSpec(memory_space=pltpu.SMEM)
    ops = left + right
    result = pl.pallas_call(
        kernel,
        out_shape=jax.ShapeDtypeStruct((16, W, W), jnp.float32),
        in_specs=[smem] * 3 + [any_space] * (1 + len(ops)),
        out_specs=pl.BlockSpec(memory_space=pltpu.VMEM),
        scratch_shapes=[
            pltpu.VMEM((STEPS, 33 * W, W), jnp.bfloat16),
            pltpu.VMEM((STEPS, 33 * W, W), jnp.bfloat16),
            pltpu.VMEM((16, 16, W), jnp.bfloat16),
            pltpu.VMEM((12, 16, W), jnp.bfloat16),
            pltpu.VMEM((8, W), jnp.int32),
            pltpu.SMEM((8, W), jnp.int32),
            pltpu.VMEM((STEPS, DENSE, DENSE), jnp.bfloat16),
            pltpu.VMEM((STEPS, 4, DENSE, 2 * W), jnp.bfloat16),
            pltpu.VMEM((H, DENSE, W), jnp.float32),
            pltpu.SemaphoreType.DMA((64,)),
        ],
        compiler_params=pltpu.CompilerParams(vmem_limit_bytes=48 * 1024 * 1024),
    )(table, cells, meta, x_blocks.reshape(4 * ROWS, W), *ops)
    return result[None, None]


def solution(mesh):
    return jax.shard_map(
        functools.partial(body, tuple(mesh.shape[a] for a in AXES)),
        mesh=mesh,
        in_specs=(P("col", "row", None, None, None), P("col", "row", None, None)),
        out_specs=P("col", "row", "layer", None, None),
        check_vma=False,
    )
```

```python
import functools

import jax
import jax.numpy as jnp
from jax import lax
from jax.experimental import pallas as pl
from jax.experimental.pallas import tpu as pltpu
from jax.sharding import PartitionSpec as P

H = 8
STEPS = 4
W = 128
HEAD = 16
TILE = 32 * W
HALF = TILE // 2
LONG = HALF + HEAD
PACK = TILE + HEAD
DENSE = H * W
AXES = ("layer", "row", "col")
BF = jnp.bfloat16


def pairs_of(mesh_shape, target):
    layers, rows, cols = mesh_shape
    flat = lambda at: (at[0] * rows + at[1]) * cols + at[2]
    found = []
    for l in range(layers):
        for r in range(rows):
            for c in range(cols):
                to = target(l, r, c)
                if to is not None:
                    found.append((flat((l, r, c)), flat(to)))
    return found


def is_relay(l, r):
    return r % 2 == l


def from_root(r, c):
    return ((r - c) // 4) % 4


def cells_and_table(coords):
    slots = coords.shape[1]
    values = jnp.arange(W, dtype=jnp.int32)
    used = jnp.any(coords[:, :, None] == values[None, None, :], axis=1)
    below = used[:, None, :] & (values[None, None, :] < coords[:, :, None])
    rank = jnp.sum(below.astype(jnp.int32), axis=2)
    cells = jnp.where(coords[0] >= 0, rank[0] * H + rank[1], H * H)
    hits = cells[None, :] == values[:, None]
    order = jnp.arange(slots, dtype=jnp.int32) - slots
    table = slots + jnp.sum(jnp.where(hits, order[None, :], 0), axis=1)
    return cells, table


class Loads:
    def __init__(self, sems):
        self.sems, self.count = sems, 0

    def start(self, choices, dst):
        sem = self.sems.at[self.count]
        self.count += 1
        for holds, src in choices:
            if holds is None:
                pltpu.make_async_copy(src, dst, sem).start()
            else:
                @pl.when(holds)
                def _():
                    pltpu.make_async_copy(src, dst, sem).start()
        src = choices[0][1]
        return lambda: pltpu.make_async_copy(src, dst, sem).wait()


def load_tile(loads, choices, tiles, heads, at, head_at):
    return [
        loads.start([(h, src.at[pl.ds(0, TILE)]) for h, src in choices], tiles.at[at, pl.ds(0, TILE)]),
        loads.start([(h, src.at[pl.ds(TILE, HEAD)]) for h, src in choices], heads.at[head_at]),
    ]


def read_tables(own_table, heads, table_v, table_s, sem):
    for i, head in enumerate(heads):
        if head is None:
            table_v[i:i + 1, :] = jnp.zeros((1, W), jnp.int32)
        else:
            table_v[i:i + 1, :] = head[0:1, :].astype(jnp.float32).astype(jnp.int32)
    copy = pltpu.make_async_copy(table_v, table_s, sem)
    copy.start()
    copy.wait()
    for i, head in enumerate(heads):
        if head is None:
            @pl.loop(0, H * H)
            def _(j):
                table_s[i, j] = own_table[j]


def add_product(a_ref, b_ref, a_row, b_row, table_s, cells, base, out):
    def block_of(ref, at, cell):
        return ref[pl.ds(pl.multiple_of(table_s[at, cell] * W, W), W), :]

    @pl.loop(0, 16, unroll=2)
    def _(q):
        cell = cells[base + q]
        held = jnp.minimum(cell, H * H - 1)
        r, c = held // H, held % H
        left = jnp.concatenate([block_of(a_ref, a_row, r * H + k) for k in range(H)], axis=1)
        right = jnp.concatenate([block_of(b_ref, b_row, k * H + c) for k in range(H)], axis=0)
        block = jnp.dot(left, right, preferred_element_type=jnp.float32)
        out[q] += jnp.where(cell < H * H, block, jnp.zeros_like(block))


def some_kernel(count, first, own_table, cells, meta, own, *refs):
    before, refs = (None, refs) if first == 0 else (refs[0], refs[1:])
    lefts, (b1r, b1s, b2r, b2s), refs = refs[:count], refs[count:count + 4], refs[count + 4:]
    out, a_all, b_all, heads, table_v, table_s, sems = refs
    relay = meta[0] == 1
    spread = meta[0] == 0
    loads = Loads(sems)
    waits = [loads.start([(None, own)], b_all.at[0, pl.ds(0, TILE)])]
    for i, src in enumerate(lefts):
        waits += load_tile(loads, [(None, src)], a_all, heads, i, 2 + i)
    for s, (on_relay, on_spread) in enumerate(((b1r, b1s), (b2r, b2s)), 1):
        waits += load_tile(loads, [(spread, on_spread), (relay, on_relay)], b_all, heads, s, s - 1)
    for i in range(count):
        a_all[i, TILE:, :] = jnp.zeros((W, W), BF)
    for i in range(3):
        b_all[i, TILE:, :] = jnp.zeros((W, W), BF)
    out[...] = jnp.zeros_like(out) if before is None else before[...]
    for wait in waits:
        wait()
    rows = [None] + [heads.at[i] for i in range(2 + count)]
    read_tables(own_table, rows, table_v, table_s, sems.at[loads.count])

    @pl.loop(0, count)
    def _(i):
        step = meta[1 + first + i]

        @pl.when(step < 3)
        def _():
            add_product(a_all.at[i], b_all.at[step], 3 + i, step, table_s, cells, meta[5], out)


def late_kernel(own_table, cells, meta, own, before, t0, t1, t2, t3, b1r, b1s, b2r, b2s, b3r, b3s,
                out, a_all, b_all, heads, table_v, table_s, sems):
    relay = meta[0] == 1
    spread = meta[0] == 0
    far_step = meta[4]
    loads = Loads(sems)
    waits = load_tile(loads, [(None, t3)], a_all, heads, 0, 0)
    choices = []
    for i, src in enumerate((t0, t1, t2)):
        holds = meta[1 + i] == 3
        choices.append((jnp.logical_or(holds, far_step == 3) if i == 0 else holds, src))
    waits += load_tile(loads, choices, a_all, heads, 1, 1)
    waits += load_tile(loads, [(spread, b3s), (relay, b3r)], b_all, heads, 1, 3)
    tiles, tops = [(far_step == 0, own)], [(far_step == 0, b1r.at[pl.ds(TILE, HEAD)])]
    for s, (on_relay, on_spread) in enumerate(((b1r, b1s), (b2r, b2s), (b3r, b3s)), 1):
        for role, src in ((relay, on_relay), (spread, on_spread)):
            holds = jnp.logical_and(role, far_step == s)
            tiles.append((holds, src.at[pl.ds(0, TILE)]))
            tops.append((holds, src.at[pl.ds(TILE, HEAD)]))
    waits.append(loads.start(tiles, b_all.at[0, pl.ds(0, TILE)]))
    waits.append(loads.start(tops, heads.at[2]))
    for i in range(2):
        a_all[i, TILE:, :] = jnp.zeros((W, W), BF)
        b_all[i, TILE:, :] = jnp.zeros((W, W), BF)
    out[...] = before[...]
    for wait in waits:
        wait()
    read_tables(own_table, [heads.at[0], heads.at[1], heads.at[2], heads.at[3], None], table_v, table_s, sems.at[loads.count])

    @pl.loop(0, 2)
    def _(i):
        @pl.when((i == 0) | (far_step < 3))
        def _():
            b_row = jnp.where((i == 0) & (far_step == 0), 4, 2 + i)
            add_product(a_all.at[i], b_all.at[i], i, b_row, table_s, cells, meta[5], out)


def call(kernel, lefts, rights, us, smem_ops, vmem_ops, any_ops):
    smem = pl.BlockSpec(memory_space=pltpu.SMEM)
    vmem = pl.BlockSpec(memory_space=pltpu.VMEM)
    anywhere = pl.BlockSpec(memory_space=pl.ANY)
    return pl.pallas_call(
        kernel,
        out_shape=jax.ShapeDtypeStruct((16, W, W), jnp.float32),
        in_specs=[smem] * len(smem_ops) + [anywhere] + [vmem] * len(vmem_ops) + [anywhere] * (len(any_ops) - 1),
        out_specs=vmem,
        scratch_shapes=[
            pltpu.VMEM((lefts, TILE + W, W), BF),
            pltpu.VMEM((rights, TILE + W, W), BF),
            pltpu.VMEM((5, HEAD, W), BF),
            pltpu.VMEM((8, W), jnp.int32),
            pltpu.SMEM((8, W), jnp.int32),
            pltpu.SemaphoreType.DMA((24,)),
        ],
        compiler_params=pltpu.CompilerParams(vmem_limit_bytes=24 * 1024 * 1024),
        cost_estimate=pl.CostEstimate(flops=int(us * 1.15e9), bytes_accessed=0, transcendentals=0),
    )(*smem_ops, any_ops[0], *vmem_ops, *any_ops[1:])


def body(mesh_shape, x_blocks, x_coords):
    tile = x_blocks.reshape(TILE, W)
    coords = x_coords[0, 0]
    rows, cols = mesh_shape[1:]
    layer, row, col = (lax.axis_index(a) for a in AXES)

    def send(value, target):
        return lax.ppermute(value, AXES, pairs_of(mesh_shape, target))

    def after(value, *others):
        return lax.optimization_barrier((value, *others))[0]

    cells, table = cells_and_table(coords)
    head = jnp.broadcast_to(table.astype(BF)[None, :], (HEAD, W))
    full = after(jnp.concatenate([tile, head]))

    low = after(tile[:LONG])
    high = after(full[HALF:])

    down = lambda l, r, c: (l, r, (c - 1) % cols) if is_relay(l, r) else None
    over = lambda l, r, c: (1 - l, r, c) if is_relay(l, r) else None
    twin = lambda l, r, c: (l, r ^ 1, c)
    cross = lambda l, r, c: (1 - l, r ^ 2, c)

    def y_hop(starts, by):
        return lambda l, r, c: (l, (r + 4 * by) % rows, c) if from_root(r, c) in starts else None

    away = from_root(row, col)
    z1 = send(full, down)
    up1 = send(low, y_hop((0,), 1))
    dn1 = send(high, y_hop((0,), -1))
    x1 = send(z1, over)
    up2 = send(jnp.where(away == 0, high, up1), y_hop((0, 1), 1))
    dn2 = send(jnp.where(away == 0, low, dn1), y_hop((0, 3), -1))
    z2 = send(z1, down)
    first = jnp.where(away == 0, low, jnp.where(away == 1, up1, jnp.where(away == 2, up2, dn2)))
    second = jnp.where(away == 0, high, jnp.where(away == 1, up2, jnp.where(away == 2, dn2, dn1)))
    t0 = after(jnp.concatenate([first[:HALF], second]))
    t2 = send(t0, cross)
    t1 = send(t0, twin)
    z3 = send(after(z2, x1), down)
    x2 = send(z2, over)
    x3 = send(after(z3, x2), over)
    t3 = send(after(t2, t1), twin)

    steps = [((row ^ bit) - col) % 4 for bit in (0, 1, 2, 3)]
    meta = jnp.stack([(row % 2 == layer).astype(jnp.int32)] + steps + [16 * layer]).astype(jnp.int32)
    small = (table, cells, meta)
    near = (z1, x1, z2, x2)
    early = call(functools.partial(some_kernel, 2, 0), 2, 3, 20, small, (), (tile, t0, t1, *near))
    middle = call(functools.partial(some_kernel, 1, 2), 1, 3, 5, small, (early,), (tile, t2, *near))
    out = call(late_kernel, 2, 2, 10, small, (middle,), (tile, t0, t1, t2, t3, *near, z3, x3))
    return out[None, None]


def solution(mesh):
    return jax.shard_map(
        functools.partial(body, tuple(mesh.shape[a] for a in AXES)),
        mesh=mesh,
        in_specs=(P("col", "row", None, None, None), P("col", "row", None, None)),
        out_specs=P("col", "row", "layer", None, None),
        check_vma=False,
    )
```

```python
import functools

import jax
import jax.numpy as jnp
from jax import lax
from jax.experimental import pallas as pl
from jax.experimental.pallas import tpu as pltpu
from jax.sharding import PartitionSpec as P

H = 8
STEPS = 4
W = 128
HEAD = 16
TILE = 32 * W
HALF = TILE // 2
LONG = HALF + HEAD
PACK = TILE + HEAD
DENSE = H * W
AXES = ("layer", "row", "col")
BF = jnp.bfloat16


def pairs_of(mesh_shape, target):
    layers, rows, cols = mesh_shape
    flat = lambda at: (at[0] * rows + at[1]) * cols + at[2]
    found = []
    for l in range(layers):
        for r in range(rows):
            for c in range(cols):
                to = target(l, r, c)
                if to is not None:
                    found.append((flat((l, r, c)), flat(to)))
    return found


def is_relay(l, r):
    return r % 2 == l


def from_root(r, c):
    return ((r - c) // 4) % 4


def cells_and_table(coords):
    slots = coords.shape[1]
    values = jnp.arange(W, dtype=jnp.int32)
    used = jnp.any(coords[:, :, None] == values[None, None, :], axis=1)
    below = used[:, None, :] & (values[None, None, :] < coords[:, :, None])
    rank = jnp.sum(below.astype(jnp.int32), axis=2)
    cells = jnp.where(coords[0] >= 0, rank[0] * H + rank[1], H * H)
    hits = cells[None, :] == values[:, None]
    order = jnp.arange(slots, dtype=jnp.int32) - slots
    table = slots + jnp.sum(jnp.where(hits, order[None, :], 0), axis=1)
    return cells, table


def add_product(a_ref, b_ref, a_row, b_row, table_s, cells, base, out):
    def block_of(ref, at, cell):
        return ref[pl.ds(pl.multiple_of(table_s[at, cell] * W, W), W), :]

    @pl.loop(0, 16, unroll=4)
    def _(q):
        cell = cells[base + q]
        held = jnp.minimum(cell, H * H - 1)
        r, c = held // H, held % H
        left = jnp.concatenate([block_of(a_ref, a_row, r * H + k) for k in range(H)], axis=1)
        right = jnp.concatenate([block_of(b_ref, b_row, k * H + c) for k in range(H)], axis=0)
        block = jnp.dot(left, right, preferred_element_type=jnp.float32)
        out[q] += jnp.where(cell < H * H, block, jnp.zeros_like(block))


def product_kernel(jobs, lefts, last_step, has_before, own_table, cells, meta, own, *refs):
    before, refs = (refs[0], refs[1:]) if has_before else (None, refs)
    tiles, refs = refs[:lefts], refs[lefts:]
    rights, refs = refs[:2 * last_step], refs[2 * last_step:]
    out, a_all, b_all, heads, table_v, table_s, sems = refs
    relay = meta[0] == 1
    spread = meta[0] == 0
    steps = [meta[1 + i] for i in range(4)]
    plans = [job(steps) for job in jobs]
    actives = []
    for j, (choices, step) in enumerate(plans):
        active = choices[0][0]
        for holds, _ in choices[1:]:
            active = jnp.logical_or(active, holds)
        actives.append(active)

        def start(src, at, row, holds):
            @pl.when(holds)
            def _():
                pltpu.make_async_copy(src.at[pl.ds(0, TILE)], at.at[j, pl.ds(0, TILE)], sems.at[row]).start()
                pltpu.make_async_copy(src.at[pl.ds(TILE, HEAD)], heads.at[row], sems.at[2 * len(plans) + row]).start()

        for holds, i in choices:
            start(tiles[i], a_all, 2 * j, holds)

        if isinstance(step, int):
            start(rights[2 * step - 2], b_all, 2 * j + 1, jnp.logical_and(active, relay))
            start(rights[2 * step - 1], b_all, 2 * j + 1, jnp.logical_and(active, spread))
            continue

        @pl.when(jnp.logical_and(active, step == 0))
        def _():
            pltpu.make_async_copy(own, b_all.at[j, pl.ds(0, TILE)], sems.at[2 * j + 1]).start()
            pltpu.make_async_copy(tiles[0].at[pl.ds(TILE, HEAD)], heads.at[2 * j + 1], sems.at[2 * len(plans) + 2 * j + 1]).start()

        for s in range(1, last_step + 1):
            holds = jnp.logical_and(active, step == s)
            start(rights[2 * s - 2], b_all, 2 * j + 1, jnp.logical_and(holds, relay))
            start(rights[2 * s - 1], b_all, 2 * j + 1, jnp.logical_and(holds, spread))

    def wait(row, at):
        pltpu.make_async_copy(own, at.at[row // 2, pl.ds(0, TILE)], sems.at[row]).wait()

    for j in range(len(plans)):
        a_all[j, TILE:, :] = jnp.zeros((W, W), BF)
        b_all[j, TILE:, :] = jnp.zeros((W, W), BF)
    out[...] = jnp.zeros_like(out) if before is None else before[...]
    table_v[...] = jnp.zeros_like(table_v)
    for j, active in enumerate(actives):
        @pl.when(active)
        def _():
            for row in (2 * j, 2 * j + 1):
                pltpu.make_async_copy(own.at[pl.ds(0, HEAD)], heads.at[row], sems.at[2 * len(plans) + row]).wait()
                table_v[row:row + 1, :] = heads[row, 0:1, :].astype(jnp.float32).astype(jnp.int32)
    copy = pltpu.make_async_copy(table_v, table_s, sems.at[4 * len(plans)])
    copy.start()
    copy.wait()
    for j, ((_, step), active) in enumerate(zip(plans, actives)):
        if not isinstance(step, int):
            @pl.when(jnp.logical_and(active, step == 0))
            def _():
                @pl.loop(0, H * H)
                def _(i):
                    table_s[2 * j + 1, i] = own_table[i]

        @pl.when(active)
        def _():
            wait(2 * j, a_all)
            wait(2 * j + 1, b_all)
            add_product(a_all.at[j], b_all.at[j], 2 * j, 2 * j + 1, table_s, cells, meta[5], out)


def pick_kernel(meta, *refs):
    lows, highs, out, sems = refs[:4], refs[4:8], refs[8], refs[9]
    for away in range(4):
        @pl.when(meta[6] == away)
        def _():
            one = pltpu.make_async_copy(lows[away].at[pl.ds(0, HALF)], out.at[pl.ds(0, HALF)], sems.at[0])
            two = pltpu.make_async_copy(highs[away], out.at[pl.ds(HALF, LONG)], sems.at[1])
            one.start()
            two.start()
            one.wait()
            two.wait()


def pack_kernel(tile, head, out, sems):
    one = pltpu.make_async_copy(tile, out.at[pl.ds(0, TILE)], sems.at[0])
    two = pltpu.make_async_copy(head, out.at[pl.ds(TILE, HEAD)], sems.at[1])
    one.start()
    two.start()
    one.wait()
    two.wait()


SMEM = pl.BlockSpec(memory_space=pltpu.SMEM)
VMEM = pl.BlockSpec(memory_space=pltpu.VMEM)
ANY = pl.BlockSpec(memory_space=pl.ANY)


def cost(us):
    return pl.CostEstimate(flops=int(us * 1.15e9), bytes_accessed=0, transcendentals=0)


def same_kernel(ref, out):
    del ref, out


def held(value, us):
    return pl.pallas_call(
        same_kernel,
        out_shape=jax.ShapeDtypeStruct(value.shape, value.dtype),
        in_specs=[ANY],
        out_specs=ANY,
        input_output_aliases={0: 0},
        cost_estimate=cost(us),
    )(value)


def pack(tile, head):
    return pl.pallas_call(
        pack_kernel,
        out_shape=jax.ShapeDtypeStruct((PACK, W), BF),
        in_specs=[ANY] * 2,
        out_specs=VMEM,
        scratch_shapes=[pltpu.SemaphoreType.DMA((2,))],
        compiler_params=pltpu.CompilerParams(vmem_limit_bytes=4 * 1024 * 1024),
        cost_estimate=cost(0.1),
    )(tile, head)


def pick(meta, lows, highs):
    return pl.pallas_call(
        pick_kernel,
        out_shape=jax.ShapeDtypeStruct((PACK, W), BF),
        in_specs=[SMEM] + [ANY] * 8,
        out_specs=VMEM,
        scratch_shapes=[pltpu.SemaphoreType.DMA((2,))],
        compiler_params=pltpu.CompilerParams(vmem_limit_bytes=4 * 1024 * 1024),
        cost_estimate=cost(10),
    )(meta, *lows, *highs)


def products(jobs, us, small, tile, before, tiles, rights):
    n = len(jobs)
    kernel = functools.partial(product_kernel, jobs, len(tiles), len(rights) // 2, len(before))
    return pl.pallas_call(
        kernel,
        out_shape=jax.ShapeDtypeStruct((16, W, W), jnp.float32),
        in_specs=[SMEM] * len(small) + [ANY] + [VMEM] * len(before) + [ANY] * (len(tiles) + len(rights)),
        out_specs=VMEM,
        scratch_shapes=[
            pltpu.VMEM((n, TILE + W, W), BF),
            pltpu.VMEM((n, TILE + W, W), BF),
            pltpu.VMEM((2 * n, HEAD, W), BF),
            pltpu.VMEM((8, W), jnp.int32),
            pltpu.SMEM((8, W), jnp.int32),
            pltpu.SemaphoreType.DMA((4 * n + 1,)),
        ],
        compiler_params=pltpu.CompilerParams(vmem_limit_bytes=16 * 1024 * 1024),
        cost_estimate=cost(0.1),
    )(*small, tile, *before, *tiles, *rights)


def body(mesh_shape, x_blocks, x_coords):
    tile = x_blocks.reshape(TILE, W)
    coords = x_coords[0, 0]
    rows, cols = mesh_shape[1:]
    layer, row, col = (lax.axis_index(a) for a in AXES)

    def send(value, target):
        return lax.ppermute(value, AXES, pairs_of(mesh_shape, target))

    def after(value, *others):
        return lax.optimization_barrier((value, *others))[0]

    cells, table = cells_and_table(coords)
    head = jnp.broadcast_to(table.astype(BF)[None, :], (HEAD, W))
    low = after(tile[:LONG])
    high = after(jnp.concatenate([tile[HALF:], head]))
    full = pack(after(tile, low, high), head)

    down = lambda l, r, c: (l, r, (c - 1) % cols) if is_relay(l, r) else None
    over = lambda l, r, c: (1 - l, r, c) if is_relay(l, r) else None
    twin = lambda l, r, c: (l, r ^ 1, c)
    cross = lambda l, r, c: (1 - l, r ^ 2, c)

    def y_hop(starts, by):
        return lambda l, r, c: (l, (r + 4 * by) % rows, c) if from_root(r, c) in starts else None

    steps = [((row ^ bit) - col) % 4 for bit in (0, 1, 2, 3)]
    meta = jnp.stack([(row % 2 == layer).astype(jnp.int32)] + steps + [16 * layer, from_root(row, col)]).astype(jnp.int32)
    small = (table, cells, meta)

    low_up = send(low, y_hop((0,), 1))
    high_dn = send(high, y_hop((0,), -1))
    z1 = send(full, down)
    high_up = send(after(high, low_up), y_hop((0,), 1))
    low_dn = send(after(low, high_dn), y_hop((0,), -1))
    z2 = send(z1, down)
    x1 = send(z1, over)
    low_far = send(low_up, y_hop((1,), 1))
    high_far = send(high_dn, y_hop((3,), -1))
    z3 = send(z2, down)
    x2 = send(after(z2, x1), over)
    t0 = pick(meta, (low, low_up, after(low_far), low_dn), (high, high_up, high_far, high_dn))
    t2 = held(send(t0, cross), 5)
    t1 = send(t0, twin)
    x3 = send(z3, over)
    first = products([lambda s: ([(s[0] < 2, 0)], s[0]), lambda s: ([(s[1] < 2, 1)], s[1])], 0.1, small, tile, (), (t0, after(t1, z3, x2)), (z1, x1))
    t3 = send(after(t2, first), twin)
    second = products([lambda s: ([(s[0] == 2, 0), (s[1] == 2, 1)], 2), lambda s: ([(s[2] < 3, 2)], s[2])], 8, small, tile, (first,), (t0, t1, t2), (z1, x1, z2, x2))
    third = products([lambda s: ([(s[i] == 3, i) for i in range(3)], 3)], 5, small, tile, (second,), (t0, t1, t2), (z1, x1, z2, x2, z3, x3))
    out = products([lambda s: ([(s[3] >= 0, 0)], s[3])], 5, small, tile, (third,), (t3,), (z1, x1, z2, x2, z3, x3))
    return out[None, None]


def solution(mesh):
    return jax.shard_map(
        functools.partial(body, tuple(mesh.shape[a] for a in AXES)),
        mesh=mesh,
        in_specs=(P("col", "row", None, None, None), P("col", "row", None, None)),
        out_specs=P("col", "row", "layer", None, None),
        check_vma=False,
    )
```

```python
import functools

import jax
import jax.numpy as jnp
from jax import lax
from jax.experimental import pallas as pl
from jax.experimental.pallas import tpu as pltpu
from jax.sharding import PartitionSpec as P

H = 8
STEPS = 4
W = 128
HEAD = 16
TILE = 32 * W
HALF = TILE // 2
LONG = HALF + HEAD
PACK = TILE + HEAD
DENSE = H * W
AXES = ("layer", "row", "col")
BF = jnp.bfloat16


def pairs_of(mesh_shape, target):
    layers, rows, cols = mesh_shape
    flat = lambda at: (at[0] * rows + at[1]) * cols + at[2]
    found = []
    for l in range(layers):
        for r in range(rows):
            for c in range(cols):
                to = target(l, r, c)
                if to is not None:
                    found.append((flat((l, r, c)), flat(to)))
    return found


def is_relay(l, r):
    return r % 2 == l


def from_root(r, c):
    return ((r - c) // 4) % 4


def cells_and_table(coords):
    slots = coords.shape[1]
    values = jnp.arange(W, dtype=jnp.int32)
    used = jnp.any(coords[:, :, None] == values[None, None, :], axis=1)
    below = used[:, None, :] & (values[None, None, :] < coords[:, :, None])
    rank = jnp.sum(below.astype(jnp.int32), axis=2)
    cells = jnp.where(coords[0] >= 0, rank[0] * H + rank[1], H * H)
    hits = cells[None, :] == values[:, None]
    order = jnp.arange(slots, dtype=jnp.int32) - slots
    table = slots + jnp.sum(jnp.where(hits, order[None, :], 0), axis=1)
    return cells, table


def add_product(a_ref, b_ref, a_row, b_row, table_s, cells, base, out):
    def block_of(ref, at, cell):
        return ref[pl.ds(pl.multiple_of(table_s[at, cell] * W, W), W), :]

    @pl.loop(0, 16, unroll=8)
    def _(q):
        cell = cells[base + q]
        held = jnp.minimum(cell, H * H - 1)
        r, c = held // H, held % H
        left = jnp.concatenate([block_of(a_ref, a_row, r * H + k) for k in range(H)], axis=1)
        right = jnp.concatenate([block_of(b_ref, b_row, k * H + c) for k in range(H)], axis=0)
        block = jnp.dot(left, right, preferred_element_type=jnp.float32)
        out[q] += jnp.where(cell < H * H, block, jnp.zeros_like(block))


CUT = 4


def spread_copies(src, dst, rows, sem):
    part = rows // CUT
    return [pltpu.make_async_copy(src.at[pl.ds(i * part, part)], dst.at[pl.ds(i * part, part)], sem) for i in range(CUT)]


def product_kernel(jobs, lefts, last_step, has_before, stored, own_table, cells, meta, own, *refs):
    before, refs = (refs[0], refs[1:]) if has_before else (None, refs)
    tiles, refs = refs[:lefts], refs[lefts:]
    rights, refs = refs[:2 * last_step], refs[2 * last_step:]
    out, a_all, b_all, heads, table_v, table_s, sems = refs
    if has_before and stored:
        for copy in spread_copies(before, out, 16, sems.at[4 * len(jobs) + 1]):
            copy.start()
    relay = meta[0] == 1
    spread = meta[0] == 0
    steps = [meta[1 + i] for i in range(4)]
    plans = [job(steps) for job in jobs]
    actives = []
    for j, (choices, step) in enumerate(plans):
        active = choices[0][0]
        for holds, _ in choices[1:]:
            active = jnp.logical_or(active, holds)
        actives.append(active)

        def start(src, at, row, holds):
            @pl.when(holds)
            def _():
                for copy in spread_copies(src, at.at[j], TILE, sems.at[row]):
                    copy.start()
                pltpu.make_async_copy(src.at[pl.ds(TILE, HEAD)], heads.at[row], sems.at[2 * len(plans) + row]).start()

        for holds, i in choices:
            start(tiles[i], a_all, 2 * j, holds)

        if isinstance(step, int):
            start(rights[2 * step - 2], b_all, 2 * j + 1, jnp.logical_and(active, relay))
            start(rights[2 * step - 1], b_all, 2 * j + 1, jnp.logical_and(active, spread))
            continue

        @pl.when(jnp.logical_and(active, step == 0))
        def _():
            for copy in spread_copies(own, b_all.at[j], TILE, sems.at[2 * j + 1]):
                copy.start()
            pltpu.make_async_copy(tiles[0].at[pl.ds(TILE, HEAD)], heads.at[2 * j + 1], sems.at[2 * len(plans) + 2 * j + 1]).start()

        for s in range(1, last_step + 1):
            holds = jnp.logical_and(active, step == s)
            start(rights[2 * s - 2], b_all, 2 * j + 1, jnp.logical_and(holds, relay))
            start(rights[2 * s - 1], b_all, 2 * j + 1, jnp.logical_and(holds, spread))

    def wait(row, at):
        pltpu.make_async_copy(own, at.at[row // 2, pl.ds(0, TILE)], sems.at[row]).wait()

    for j in range(len(plans)):
        a_all[j, TILE:, :] = jnp.zeros((W, W), BF)
        b_all[j, TILE:, :] = jnp.zeros((W, W), BF)
    if before is None:
        out[...] = jnp.zeros_like(out)
    elif not stored:
        out[...] = before[...]
    table_v[...] = jnp.zeros_like(table_v)
    for j, active in enumerate(actives):
        @pl.when(active)
        def _():
            for row in (2 * j, 2 * j + 1):
                pltpu.make_async_copy(own.at[pl.ds(0, HEAD)], heads.at[row], sems.at[2 * len(plans) + row]).wait()
                table_v[row:row + 1, :] = heads[row, 0:1, :].astype(jnp.float32).astype(jnp.int32)
    copy = pltpu.make_async_copy(table_v, table_s, sems.at[4 * len(plans)])
    copy.start()
    copy.wait()
    if has_before and stored:
        pltpu.make_async_copy(before, out, sems.at[4 * len(jobs) + 1]).wait()
    for j, ((_, step), active) in enumerate(zip(plans, actives)):
        if not isinstance(step, int):
            @pl.when(jnp.logical_and(active, step == 0))
            def _():
                @pl.loop(0, H * H)
                def _(i):
                    table_s[2 * j + 1, i] = own_table[i]

        @pl.when(active)
        def _():
            wait(2 * j, a_all)
            wait(2 * j + 1, b_all)
            add_product(a_all.at[j], b_all.at[j], 2 * j, 2 * j + 1, table_s, cells, meta[5], out)


def pick_kernel(meta, *refs):
    lows, highs, out, sems = refs[:4], refs[4:8], refs[8], refs[9]
    for away in range(4):
        @pl.when(meta[6] == away)
        def _():
            copies = spread_copies(lows[away], out, HALF, sems.at[0])
            copies += spread_copies(highs[away], out.at[pl.ds(HALF, HALF)], HALF, sems.at[1])
            copies.append(pltpu.make_async_copy(highs[away].at[pl.ds(HALF, HEAD)], out.at[pl.ds(TILE, HEAD)], sems.at[2]))
            for copy in copies:
                copy.start()
    pltpu.make_async_copy(lows[0].at[pl.ds(0, HALF)], out.at[pl.ds(0, HALF)], sems.at[0]).wait()
    pltpu.make_async_copy(highs[0].at[pl.ds(0, HALF)], out.at[pl.ds(HALF, HALF)], sems.at[1]).wait()
    pltpu.make_async_copy(highs[0].at[pl.ds(HALF, HEAD)], out.at[pl.ds(TILE, HEAD)], sems.at[2]).wait()


def pack_kernel(tile, head, out, sems):
    copies = spread_copies(tile, out, TILE, sems.at[0])
    copies.append(pltpu.make_async_copy(head, out.at[pl.ds(TILE, HEAD)], sems.at[1]))
    for copy in copies:
        copy.start()
    pltpu.make_async_copy(tile, out.at[pl.ds(0, TILE)], sems.at[0]).wait()
    copies[-1].wait()


SMEM = pl.BlockSpec(memory_space=pltpu.SMEM)
VMEM = pl.BlockSpec(memory_space=pltpu.VMEM)
ANY = pl.BlockSpec(memory_space=pl.ANY)
HBM = pl.BlockSpec(memory_space=pltpu.HBM)


def cost(us):
    return pl.CostEstimate(flops=int(us * 1.15e9), bytes_accessed=0, transcendentals=0)


def same_kernel(ref, out):
    del ref, out


def held(value, us):
    return pl.pallas_call(
        same_kernel,
        out_shape=jax.ShapeDtypeStruct(value.shape, value.dtype),
        in_specs=[ANY],
        out_specs=ANY,
        input_output_aliases={0: 0},
        cost_estimate=cost(us),
    )(value)


def pack(tile, head):
    return pl.pallas_call(
        pack_kernel,
        out_shape=jax.ShapeDtypeStruct((PACK, W), BF),
        in_specs=[ANY] * 2,
        out_specs=VMEM,
        scratch_shapes=[pltpu.SemaphoreType.DMA((3,))],
        compiler_params=pltpu.CompilerParams(vmem_limit_bytes=4 * 1024 * 1024),
        cost_estimate=cost(0.1),
    )(tile, head)


def pick(meta, lows, highs):
    return pl.pallas_call(
        pick_kernel,
        out_shape=jax.ShapeDtypeStruct((PACK, W), BF),
        in_specs=[SMEM] + [ANY] * 8,
        out_specs=VMEM,
        scratch_shapes=[pltpu.SemaphoreType.DMA((3,))],
        compiler_params=pltpu.CompilerParams(vmem_limit_bytes=4 * 1024 * 1024),
        cost_estimate=cost(10),
    )(meta, *lows, *highs)


def products(jobs, us, small, tile, before, tiles, rights, stored=False, far=()):
    n = len(jobs)
    kernel = functools.partial(product_kernel, jobs, len(tiles), len(rights) // 2, len(before), stored)
    return pl.pallas_call(
        kernel,
        out_shape=jax.ShapeDtypeStruct((16, W, W), jnp.float32),
        in_specs=[SMEM] * len(small) + [ANY] + [HBM if stored else VMEM] * len(before)
        + [HBM if i in far else ANY for i in range(len(tiles))] + [ANY] * len(rights),
        out_specs=VMEM,
        scratch_shapes=[
            pltpu.VMEM((n, TILE + W, W), BF),
            pltpu.VMEM((n, TILE + W, W), BF),
            pltpu.VMEM((2 * n, HEAD, W), BF),
            pltpu.VMEM((8, W), jnp.int32),
            pltpu.SMEM((8, W), jnp.int32),
            pltpu.SemaphoreType.DMA((4 * n + 2,)),
        ],
        compiler_params=pltpu.CompilerParams(vmem_limit_bytes=16 * 1024 * 1024),
        cost_estimate=cost(0.1),
    )(*small, tile, *before, *tiles, *rights)


def body(mesh_shape, x_blocks, x_coords):
    tile = x_blocks.reshape(TILE, W)
    coords = x_coords[0, 0]
    rows, cols = mesh_shape[1:]
    layer, row, col = (lax.axis_index(a) for a in AXES)

    def send(value, target):
        return lax.ppermute(value, AXES, pairs_of(mesh_shape, target))

    def after(value, *others):
        return lax.optimization_barrier((value, *others))[0]

    cells, table = cells_and_table(coords)
    head = jnp.broadcast_to(table.astype(BF)[None, :], (HEAD, W))
    low = after(tile[:LONG])
    high = after(jnp.concatenate([tile[HALF:], head]))
    full = pack(tile, head)

    down = lambda l, r, c: (l, r, (c - 1) % cols) if is_relay(l, r) else None
    over = lambda l, r, c: (1 - l, r, c) if is_relay(l, r) else None
    twin = lambda l, r, c: (l, r ^ 1, c)
    cross = lambda l, r, c: (1 - l, r ^ 2, c)

    def y_hop(starts, by):
        return lambda l, r, c: (l, (r + 4 * by) % rows, c) if from_root(r, c) in starts else None

    steps = [((row ^ bit) - col) % 4 for bit in (0, 1, 2, 3)]
    meta = jnp.stack([(row % 2 == layer).astype(jnp.int32)] + steps + [16 * layer, from_root(row, col)]).astype(jnp.int32)
    small = (table, cells, meta)

    low_up = send(low, y_hop((0,), 1))
    high_dn = send(after(high, full), y_hop((0,), -1))
    z1 = send(full, down)
    high_up = send(after(high, low_up), y_hop((0,), 1))
    low_dn = send(after(low, high_dn), y_hop((0,), -1))
    z2 = send(z1, down)
    x1 = send(z1, over)
    low_far = send(low_up, y_hop((1,), 1))
    high_far = send(high_dn, y_hop((3,), -1))
    z3 = send(z2, down)
    x2 = send(after(z2, x1), over)
    t0 = pick(meta, (low, low_up, after(low_far), low_dn), (high, high_up, high_far, high_dn))
    t1 = send(t0, twin)
    first = products([lambda s: ([(s[0] < 2, 0)], s[0]), lambda s: ([(s[1] < 2, 1)], s[1])], 0.1, small, tile, (), (t0, t1), (z1, x1))
    t2 = held(after(send(t0, cross), first), 5)
    x3 = send(z3, over)
    t3 = send(t2, twin)
    kept0, kept1, kept = (pltpu.with_memory_space_constraint(v, pltpu.HBM) for v in (t0, t1, first))
    second = products([lambda s: ([(s[0] == 2, 0), (s[1] == 2, 1)], 2), lambda s: ([(s[2] < 3, 2)], s[2]), lambda s: ([(s[3] < 3, 3)], s[3])], 8, small, tile, (kept,), (kept0, kept1, t2, t3), (z1, x1, z2, x2), stored=True, far=(0, 1))
    out = products([lambda s: ([(s[i] == 3, i) for i in range(4)], 3)], 5, small, tile, (second,), (kept0, kept1, t2, t3), (z1, x1, z2, x2, z3, x3), far=(0, 1))
    return out[None, None]


def solution(mesh):
    return jax.shard_map(
        functools.partial(body, tuple(mesh.shape[a] for a in AXES)),
        mesh=mesh,
        in_specs=(P("col", "row", None, None, None), P("col", "row", None, None)),
        out_specs=P("col", "row", "layer", None, None),
        check_vma=False,
    )
```
